256 devices in a mesh: blk: 8 (over z), tp: 4 (over x_hi, core), rep: 8 (over x_lo, y).
Axes of the slice: x: 4 (x_hi: 2, x_lo: 2; x = x_hi * 2 + x_lo), y: 4, z: 8, core: 2. Of those that a mesh axis runs over, the one named last changes fastest.
Arguments:
- context: bfloat16 [24576, 2560], P(('blk', 'rep'), 'tp'), may hold values from -6 to 6
- out_weight: bfloat16 [5120, 2560], P('blk', 'tp'), may hold values from -0.125 to 0.125
- grad_out: bfloat16 [24576, 5120], P(('blk', 'rep'), 'tp'), may hold values from -16 to 16
Outputs:
- projected: bfloat16 [24576, 5120], P(('blk', 'rep'), 'tp')
- grad_context: bfloat16 [24576, 2560], P(('blk', 'rep'), 'tp')
- grad_weight: float32 [5120, 2560], P(('blk', 'rep'), 'tp')
The draws below stay inside these ranges and needn't reach their ends.
All inputs are finite; a program needn't handle non-finite values.
Results may differ from the reference program's by a relative error of at most 0.015.
Values may be sent and summed in bfloat16 or wider, within the bound.
No kernel may reach another device: no remote copies, remote signals or barrier semaphores. Data moves between devices by JAX's collectives and lax.ppermute only.
A program may use at most 128 MiB of HBM per device.

```python
import jax
import jax.numpy as jnp

D = 5120
HEADS = 20
HEAD = 128
HD = 2560
TOKENS = 24576
N_TP = 4


def strengthened(array, rng, source, target, shards_of, factor):
    def block_of(axis_at):
        return (jnp.arange(array.shape[axis_at]) // (array.shape[axis_at] // shards_of)).reshape((-1,) + (1,) * (array.ndim - 1 - axis_at))

    near = jax.random.permutation(rng, shards_of)[block_of(target)]
    second = (block_of(target) + shards_of // 2) % shards_of
    return jnp.where((block_of(source) == near) | (block_of(source) == second), factor * array, array)


def shard_levels(own_key, shape, shards, low, largest):
    def one(axis_at, parts):
        steps = jax.random.uniform(jax.random.fold_in(jax.random.fold_in(own_key, 6), axis_at), (parts,), jnp.float32, low / len(shards), largest / len(shards))
        return jnp.repeat(jnp.exp(steps), shape[axis_at] // parts).reshape((-1,) + (1,) * (len(shape) - axis_at - 1))

    loudness = one(*shards[0])
    for cut in shards[1:]:
        loudness = loudness * one(*cut)
    return loudness


def scatter_about(own_key, shape, spread, bound, split=(), kind=jnp.bfloat16):
    entries = spread * jax.random.normal(own_key, shape, jnp.float32)
    if split:
        entries = entries * shard_levels(own_key, shape, split, -0.22, 0.18)
    return jnp.clip(entries, -bound, bound).astype(kind)


def gaussian_with(stream_key, dims, scale, reach, split, heavy, dtype=jnp.bfloat16):
    array = scale * jax.random.normal(stream_key, dims, jnp.float32)
    if split:
        array = array * shard_levels(stream_key, dims, split, -0.22, 0.18)
    return jnp.clip(strengthened(array, jax.random.fold_in(stream_key, 3), *heavy), -reach, reach).astype(dtype)


def setup_inputs(seed: int = 0) -> dict:
    keys = jax.random.split(jax.random.key(seed), 4)
    context = scatter_about(keys[0], (TOKENS, HD), 1.0, 6.0, ((0, 64), (1, 4)))
    out_weight = scatter_about(keys[1], (D, HD), HD ** -0.5, 0.125, ((0, 8), (1, 4)))
    grad_out = gaussian_with(keys[2], (TOKENS, D), 1.0, 16.0, ((0, 64), (1, 4)), (0, 1, 64, 4.0))
    return {"context": context, "out_weight": out_weight, "grad_out": grad_out}


def reference(context, out_weight, grad_out):
    width = HEADS * HEAD // N_TP
    total = jnp.zeros((context.shape[0], out_weight.shape[0]), jnp.float32)
    for group in range(N_TP):
        left = context[:, group * width:(group + 1) * width]
        right = out_weight[:, group * width:(group + 1) * width]
        partial_value = jnp.dot(left, right.T, preferred_element_type=jnp.float32).astype(jnp.bfloat16)
        total = total + partial_value.astype(jnp.float32)
    projected = total.astype(jnp.bfloat16)
    grad_context = jnp.dot(grad_out, out_weight, preferred_element_type=jnp.float32).astype(jnp.bfloat16)
    grad_weight = jnp.dot(grad_out.T, context, preferred_element_type=jnp.float32)
    return projected, grad_context, grad_weight
```

```python
import jax
import jax.numpy as jnp
from jax import lax
from jax.sharding import PartitionSpec as P

BF, F32 = jnp.bfloat16, jnp.float32
ALL = ("blk", "tp", "rep")


def number(z, a, k, l, y):
    return (z * 4 + a * 2 + k) * 8 + l * 4 + y


def places():
    for z in range(8):
        for a in range(2):
            for k in range(2):
                for l in range(2):
                    for y in range(4):
                        yield z, a, k, l, y


def move(value, target):
    return lax.ppermute(value, ALL, [(number(*p), number(*target(*p))) for p in places()])


def core_swap(v):
    return move(v, lambda z, a, k, l, y: (z, a, 1 - k, l, y))


def x_swap(v):
    return move(v, lambda z, a, k, l, y: (z, a, k, 1 - l, y))


def dot(a, b, ca, cb):
    return lax.dot_general(a, b, (((ca,), (cb,)), ((), ())), preferred_element_type=F32)


def body(context, out_weight, grad_out):
    z = lax.axis_index("blk")
    t = lax.axis_index("tp")
    r = lax.axis_index("rep")
    a, k, h, y = t // 2, t % 2, r // 4, r % 4

    half = lax.dynamic_slice_in_dim(out_weight, h * 320, 320, 0)
    w_piece = move(half, lambda z, a, k, l, y: (2 * (z % 4) + l, z // 4, k, a, y))
    weight = lax.all_gather(w_piece, "blk", axis=0, tiled=True)

    c_a = move(context, lambda z, a, k, l, y: (z, l, k, a, y))
    c_b = move(context, lambda z, a, k, l, y: (z, 1 - l, k, a, y))
    same = a == h
    ctx = jnp.concatenate([jnp.where(same, c_a, c_b), jnp.where(same, c_b, c_a)], axis=0)

    def both(mine):
        other = core_swap(mine)
        first = k == 0
        return jnp.concatenate([jnp.where(first, mine, other), jnp.where(first, other, mine)], axis=1)

    gout_far = x_swap(grad_out)
    gout = jnp.concatenate([both(grad_out), both(gout_far)], axis=0)

    gw = dot(gout, ctx, 0, 0).astype(BF).reshape(8, 4, 80, 640)
    total = lax.dynamic_index_in_dim(gw, y, 1, keepdims=False).astype(F32)
    for d in (1, 3, 2):
        piece = lax.dynamic_index_in_dim(gw, (y + d) % 4, 1, keepdims=False)
        total += move(piece, lambda z, a, k, l, y: (z, a, k, l, (y + d) % 4)).astype(F32)
    gy = total.astype(BF)
    grad_weight = jnp.zeros((80, 640), F32)
    for d in range(8):
        piece = lax.dynamic_index_in_dim(gy, (z + d) % 8, 0, keepdims=False)

        def owner(z, a, k, l, y):
            code = (z + d) % 8
            return 4 * a + code // 2, l, k, code % 2, y

        grad_weight += move(piece, owner).astype(F32)

    part = dot(ctx, weight, 1, 1).astype(BF)
    mine = lax.dynamic_slice_in_dim(part, k * 1280, 1280, 1)
    theirs = lax.dynamic_slice_in_dim(part, (1 - k) * 1280, 1280, 1)
    half_sum = (mine.astype(F32) + core_swap(theirs).astype(F32)).astype(BF)
    projected = (half_sum[:384].astype(F32) + x_swap(half_sum[384:]).astype(F32)).astype(BF)

    gc = dot(gout, weight, 1, 0).astype(BF)
    for_a = jnp.where(same, gc[:384], gc[384:])
    for_b = jnp.where(same, gc[384:], gc[:384])
    g_a = move(for_a, lambda z, a, k, l, y: (z, l, k, a, y))
    g_b = move(for_b, lambda z, a, k, l, y: (z, l, k, 1 - a, y))
    grad_context = (g_a.astype(F32) + g_b.astype(F32)).astype(BF)
    return projected, grad_context, grad_weight


def solution(mesh):
    spec = P(("blk", "rep"), "tp")
    return jax.shard_map(
        body,
        mesh=mesh,
        in_specs=(spec, P("blk", "tp"), spec),
        out_specs=(spec, spec, spec),
        check_vma=False,
    )
```

```python
import functools

import jax
import jax.numpy as jnp
from jax import lax
from jax.experimental import pallas as pl
from jax.experimental.pallas import tpu as pltpu
from jax.sharding import PartitionSpec as P

BF, F32 = jnp.bfloat16, jnp.float32
ALL = ("blk", "tp", "rep")


def number(z, a, k, l, y):
    return (z * 4 + a * 2 + k) * 8 + l * 4 + y


def places():
    for z in range(8):
        for a in range(2):
            for k in range(2):
                for l in range(2):
                    for y in range(4):
                        yield z, a, k, l, y


def move(value, target):
    pairs = [(number(*p), number(*target(*p))) for p in places() if target(*p)]
    return lax.ppermute(value, ALL, pairs)


def swap_core(v):
    return move(v, lambda z, a, k, l, y: (z, a, 1 - k, l, y))


def swap_lo(v):
    return move(v, lambda z, a, k, l, y: (z, a, k, 1 - l, y))


def swap_hi(v):
    return move(v, lambda z, a, k, l, y: (z, 1 - a, k, l, y))


def swap_both(v):
    return move(v, lambda z, a, k, l, y: (z, 1 - a, k, 1 - l, y))


def to_pair(z, a, k, l, y):
    return (z ^ 1, a, k, l, y) if z % 2 == l else None


def to_home(z, a, k, l, y):
    return (z - z % 2 + l, a, k, z % 2, y)


def dot(a, b, ca, cb):
    return lax.dot_general(a, b, (((ca,), (cb,)), ((), ())), preferred_element_type=F32)


def add(*terms):
    total = terms[0].astype(F32)
    for term in terms[1:]:
        total = total + term.astype(F32)
    return total


def pick(v, i, axis):
    return lax.dynamic_index_in_dim(v, i, axis, keepdims=False)


def over_y(v, y):
    axis = v.ndim - 3
    got = [pick(v, y, axis)]
    for d in (1, 3, 2):
        got.append(move(pick(v, (y + d) % 4, axis), lambda z, a, k, l, y: (z, a, k, l, (y + d) % 4)))
    return add(*got)


def call(kernel, outs, flops, n_in):
    whole = pl.BlockSpec(memory_space=pltpu.VMEM)
    return pl.pallas_call(
        kernel,
        out_shape=[jax.ShapeDtypeStruct(s, BF) for s in outs],
        in_specs=[pl.BlockSpec(memory_space=pltpu.SMEM)] + [whole] * n_in,
        out_specs=[whole] * len(outs),
        compiler_params=pltpu.CompilerParams(vmem_limit_bytes=40 << 20),
        cost_estimate=pl.CostEstimate(flops=flops, bytes_accessed=8 << 20, transcendentals=0),
    )


WORK = 2 * 768 * 2560 * 640


def gw_kernel(t, *refs):
    g_own, g_far, c_own, c_far, out = refs[:4], refs[4:8], refs[8], refs[9], refs[10]
    for q in range(4):
        out[t[0] ^ q] = (dot(g_own[q][...], c_own[...], 0, 0) + dot(g_far[q][...], c_far[...], 0, 0)).astype(BF)


def proj_kernel(t, c_own, c_far, w, *outs):
    for q in (1, 3, 0, 2):
        for s, c in enumerate((c_far, c_own)):
            outs[q % 2][q // 2, s] = dot(c[...], w[t[0] ^ q], 1, 1).astype(BF)


def gc_kernel(t, *refs):
    w, far, own = refs[8:]
    for g, out in ((refs[4:8], far), (refs[:4], own)):
        total = dot(g[0][...], w[t[0]], 1, 0)
        for q in range(1, 4):
            total += dot(g[q][...], w[t[0] ^ q], 1, 0)
        out[...] = total.astype(BF)


def body(context, out_weight, grad_out):
    z = lax.axis_index("blk")
    t = lax.axis_index("tp")
    r = lax.axis_index("rep")
    f, y = r // 4, r % 4
    at = t.astype(jnp.int32).reshape(1)

    part = lax.dynamic_slice_in_dim(out_weight, (1 - f) * 320, 320, 0)
    mine = lax.dynamic_slice_in_dim(out_weight, f * 320, 320, 0)
    part = jnp.where(z % 2 == f, mine, move(part, to_pair))
    weight = lax.all_gather(part, "blk", axis=0, tiled=True)

    g_mine = lax.dynamic_slice_in_dim(grad_out, f * 640, 640, 1)
    g_theirs = lax.dynamic_slice_in_dim(grad_out, (1 - f) * 640, 640, 1)
    near = swap_lo(g_theirs)
    c_far = swap_lo(context)
    cross = swap_both(g_theirs)
    hi = swap_hi(g_mine)
    own = [g_mine, swap_core(g_mine), hi, swap_core(hi)]
    far = [near, swap_core(near), cross, swap_core(cross)]

    gw = call(gw_kernel, [(4, 640, 640)], WORK, 10)(at, *own, *far, context, c_far)[0]
    gw, weight = lax.optimization_barrier((gw, weight))
    gw = lax.psum_scatter(gw.reshape(8, 4, 80, 640), "blk", scatter_dimension=0, tiled=True)
    grad_weight = move(over_y(gw[0], y).astype(BF), to_home).astype(F32)

    w = weight.reshape(4, 640, 640)
    keep, give = call(proj_kernel, [(2, 2, 384, 640)] * 2, WORK, 3)(at, context, c_far, w)
    keep = add(keep, swap_core(give)).astype(BF)
    first = add(keep[0, 1], swap_hi(keep[1, 1])).astype(BF)
    second = add(swap_lo(keep[0, 0]), swap_both(keep[1, 0])).astype(BF)
    low = f == 0
    projected = jnp.concatenate([jnp.where(low, first, second), jnp.where(low, second, first)], axis=1)

    gc_far, gc_own = call(gc_kernel, [(384, 640)] * 2, WORK, 9)(at, *own, *far, w)
    grad_context = add(gc_own, swap_lo(gc_far)).astype(BF)
    return projected, grad_context, grad_weight


def solution(mesh):
    spec = P(("blk", "rep"), "tp")
    return jax.shard_map(
        body,
        mesh=mesh,
        in_specs=(spec, P("blk", "tp"), spec),
        out_specs=(spec, spec, spec),
        check_vma=False,
    )
```

```python
import jax
import jax.numpy as jnp
from jax import lax
from jax.experimental import pallas as pl
from jax.experimental.pallas import tpu as pltpu
from jax.sharding import PartitionSpec as P

BF, F32 = jnp.bfloat16, jnp.float32
ALL = ("blk", "tp", "rep")
WORK = 2 * 768 * 2560 * 640


def number(z, a, k, l, y):
    return (z * 4 + a * 2 + k) * 8 + l * 4 + y


def places():
    for z in range(8):
        for a in range(2):
            for k in range(2):
                for l in range(2):
                    for y in range(4):
                        yield z, a, k, l, y


def move(value, target):
    return lax.ppermute(value, ALL, [(number(*p), number(*target(*p))) for p in places()])


def swap_core(v):
    return move(v, lambda z, a, k, l, y: (z, a, 1 - k, l, y))


def swap_lo(v):
    return move(v, lambda z, a, k, l, y: (z, a, k, 1 - l, y))


def swap_hi(v):
    return move(v, lambda z, a, k, l, y: (z, 1 - a, k, l, y))


def swap_both(v):
    return move(v, lambda z, a, k, l, y: (z, 1 - a, k, 1 - l, y))


def to_y(v, d):
    return move(v, lambda z, a, k, l, y: (z, a, k, l, (y + d) % 4))


def dot(a, b, ca, cb):
    return lax.dot_general(a, b, (((ca,), (cb,)), ((), ())), preferred_element_type=F32)


def add(*terms):
    total = terms[0].astype(F32)
    for term in terms[1:]:
        total = total + term.astype(F32)
    return total


def pick(v, i, axis):
    return lax.dynamic_index_in_dim(v, i, axis, keepdims=False)


def over_y(v, y):
    return add(pick(v, y, 0), *(to_y(pick(v, (y + d) % 4, 0), d) for d in (1, 3, 2)))


def call(kernel, outs, flops, n_in):
    whole = pl.BlockSpec(memory_space=pltpu.VMEM)
    return pl.pallas_call(
        kernel,
        out_shape=[jax.ShapeDtypeStruct(s, BF) for s in outs],
        in_specs=[pl.BlockSpec(memory_space=pltpu.SMEM)] + [whole] * n_in,
        out_specs=[whole] * len(outs),
        compiler_params=pltpu.CompilerParams(vmem_limit_bytes=40 << 20),
        cost_estimate=pl.CostEstimate(flops=flops, bytes_accessed=8 << 20, transcendentals=0),
    )


def split_kernel(at, g, mine, theirs):
    for f in range(2):

        @pl.when(at[1] == f)
        def _():
            for i in range(2):
                mine[:, i * 320 : i * 320 + 320] = g[:, i * 640 + f * 320 : i * 640 + f * 320 + 320]
                theirs[:, i * 320 : i * 320 + 320] = g[:, i * 640 + 320 - f * 320 : i * 640 + 640 - f * 320]


def join_kernel(at, keep, hi, lo, both, out):
    first = (keep[0, 1].astype(F32) + hi[...].astype(F32)).astype(BF)
    second = (lo[...].astype(F32) + both[...].astype(F32)).astype(BF)
    for f in range(2):

        @pl.when(at[1] == f)
        def _():
            for i in range(2):
                out[:, i * 640 + f * 320 : i * 640 + f * 320 + 320] = first[:, i * 320 : i * 320 + 320]
                out[:, i * 640 + 320 - f * 320 : i * 640 + 640 - f * 320] = second[:, i * 320 : i * 320 + 320]


def gw_kernel(at, *refs):
    g_own, g_far, c_own, c_far, out = refs[:4], refs[4:8], refs[8], refs[9], refs[10]
    for q in range(4):
        out[at[0] ^ q] = (dot(g_own[q][...], c_own[...], 0, 0) + dot(g_far[q][...], c_far[...], 0, 0)).astype(BF)


def proj_kernel(at, c_own, c_far, w, *outs):
    for q in (1, 3, 0, 2):
        for s, c in enumerate((c_far, c_own)):
            outs[q % 2][q // 2, s] = dot(c[...], w[at[0] ^ q], 1, 1).astype(BF)


def gc_kernel(at, *refs):
    w, far, own = refs[8:]
    for g, out in ((refs[4:8], far), (refs[:4], own)):
        total = dot(g[0][...], w[at[0]], 1, 0)
        for q in range(1, 4):
            total += dot(g[q][...], w[at[0] ^ q], 1, 0)
        out[...] = total.astype(BF)


def body(context, out_weight, grad_out):
    t = lax.axis_index("tp")
    r = lax.axis_index("rep")
    f, y = r // 4, r % 4
    at = jnp.stack([t, f]).astype(jnp.int32)

    half = lax.dynamic_slice_in_dim(out_weight, f * 320, 320, 0)
    weight = lax.all_gather(half, "blk", axis=0, tiled=True)

    c_far = swap_lo(context)
    g_mine, g_theirs = call(split_kernel, [(384, 640)] * 2, 0, 1)(at, grad_out)
    near = swap_lo(g_theirs)
    cross = swap_both(g_theirs)
    hi = swap_hi(g_mine)
    own = [g_mine, swap_core(g_mine), hi, swap_core(hi)]
    far = [near, swap_core(near), cross, swap_core(cross)]

    gw = call(gw_kernel, [(4, 640, 640)], WORK, 10)(at, *own, *far, context, c_far)[0]
    gw, weight = lax.optimization_barrier((gw, weight))
    gw = lax.psum_scatter(gw.reshape(8, 4, 80, 640), "blk", scatter_dimension=0, tiled=True)
    grad_weight = over_y(gw[0], y)

    w = weight.reshape(4, 640, 640)
    keep, give = call(proj_kernel, [(2, 2, 384, 640)] * 2, WORK, 3)(at, context, c_far, w)
    keep = add(keep, swap_core(give)).astype(BF)
    parts = keep, swap_hi(keep[1, 1]), swap_lo(keep[0, 0]), swap_both(keep[1, 0])
    projected = call(join_kernel, [(384, 1280)], 0, 4)(at, *parts)[0]

    gc_far, gc_own = call(gc_kernel, [(384, 640)] * 2, WORK, 9)(at, *own, *far, w)
    grad_context = add(gc_own, swap_lo(gc_far)).astype(BF)
    return projected, grad_context, grad_weight


def solution(mesh):
    spec = P(("blk", "rep"), "tp")
    return jax.shard_map(
        body,
        mesh=mesh,
        in_specs=(spec, P("blk", "tp"), spec),
        out_specs=(spec, spec, spec),
        check_vma=False,
    )
```

```python
import jax
import jax.numpy as jnp
from jax import lax
from jax.experimental import pallas as pl
from jax.experimental.pallas import tpu as pltpu
from jax.sharding import PartitionSpec as P

BF, F32 = jnp.bfloat16, jnp.float32
ALL = ("blk", "tp", "rep")
WORK = 2 * 768 * 2560 * 640


def number(z, a, k, l, y):
    return (z * 4 + a * 2 + k) * 8 + l * 4 + y


def places():
    for z in range(8):
        for a in range(2):
            for k in range(2):
                for l in range(2):
                    for y in range(4):
                        yield z, a, k, l, y


def move(value, target):
    return lax.ppermute(value, ALL, [(number(*p), number(*target(*p))) for p in places()])


def swap_core(v):
    return move(v, lambda z, a, k, l, y: (z, a, 1 - k, l, y))


def swap_lo(v):
    return move(v, lambda z, a, k, l, y: (z, a, k, 1 - l, y))


def swap_hi(v):
    return move(v, lambda z, a, k, l, y: (z, 1 - a, k, l, y))


def swap_both(v):
    return move(v, lambda z, a, k, l, y: (z, 1 - a, k, 1 - l, y))


def to_y(v, d):
    return move(v, lambda z, a, k, l, y: (z, a, k, l, (y + d) % 4))


def dot(a, b, ca, cb):
    return lax.dot_general(a, b, (((ca,), (cb,)), ((), ())), preferred_element_type=F32)


def add(*terms):
    total = terms[0].astype(F32)
    for term in terms[1:]:
        total = total + term.astype(F32)
    return total


def pick(v, i, axis):
    return lax.dynamic_index_in_dim(v, i, axis, keepdims=False)


def over_y(v, y):
    turn = (1, 3, 2)
    mine, *pieces = lax.optimization_barrier([pick(v, (y + d) % 4, 0) for d in (0, *turn)])
    return add(mine, *(to_y(piece, d) for piece, d in zip(pieces, turn)))


def call(kernel, outs, flops, n_in):
    whole = pl.BlockSpec(memory_space=pltpu.VMEM)
    return pl.pallas_call(
        kernel,
        out_shape=[jax.ShapeDtypeStruct(s, BF) for s in outs],
        in_specs=[pl.BlockSpec(memory_space=pltpu.SMEM)] + [whole] * n_in,
        out_specs=[whole] * len(outs),
        compiler_params=pltpu.CompilerParams(vmem_limit_bytes=40 << 20),
        cost_estimate=pl.CostEstimate(flops=flops, bytes_accessed=8 << 20, transcendentals=0),
    )


def split_kernel(at, g, mine, theirs):
    for f in range(2):

        @pl.when(at[1] == f)
        def _():
            for i in range(2):
                mine[:, i * 320 : i * 320 + 320] = g[:, i * 640 + f * 320 : i * 640 + f * 320 + 320]
                theirs[:, i * 320 : i * 320 + 320] = g[:, i * 640 + 320 - f * 320 : i * 640 + 640 - f * 320]


def join_kernel(at, keep, hi, lo, both, out):
    first = (keep[0, 1].astype(F32) + hi[...].astype(F32)).astype(BF)
    second = (lo[...].astype(F32) + both[...].astype(F32)).astype(BF)
    for f in range(2):

        @pl.when(at[1] == f)
        def _():
            for i in range(2):
                out[:, i * 640 + f * 320 : i * 640 + f * 320 + 320] = first[:, i * 320 : i * 320 + 320]
                out[:, i * 640 + 320 - f * 320 : i * 640 + 640 - f * 320] = second[:, i * 320 : i * 320 + 320]


def gw_kernel(at, *refs):
    g_own, g_far, c_own, c_far, out = refs[:4], refs[4:8], refs[8], refs[9], refs[10]
    for q in range(4):
        out[at[0] ^ q] = (dot(g_own[q][...], c_own[...], 0, 0) + dot(g_far[q][...], c_far[...], 0, 0)).astype(BF)


def proj_kernel(at, c_own, c_far, w, *outs):
    for q in (1, 3, 0, 2):
        for s, c in enumerate((c_far, c_own)):
            outs[q % 2][q // 2, s] = dot(c[...], w[at[0] ^ q], 1, 1).astype(BF)


def gc_kernel(at, *refs):
    w, far, own = refs[8:]
    for g, out in ((refs[4:8], far), (refs[:4], own)):
        total = dot(g[0][...], w[at[0]], 1, 0)
        for q in range(1, 4):
            total += dot(g[q][...], w[at[0] ^ q], 1, 0)
        out[...] = total.astype(BF)


def body(context, out_weight, grad_out):
    t = lax.axis_index("tp")
    r = lax.axis_index("rep")
    f, y = r // 4, r % 4
    at = jnp.stack([t, f]).astype(jnp.int32)

    half = lax.dynamic_slice_in_dim(out_weight, f * 320, 320, 0)
    weight = lax.all_gather(half, "blk", axis=0, tiled=True)

    c_far = swap_lo(context)
    g_mine, g_theirs = call(split_kernel, [(384, 640)] * 2, 0, 1)(at, grad_out)
    near = swap_lo(g_theirs)
    cross = swap_both(g_theirs)
    hi = swap_hi(g_mine)
    own = [g_mine, swap_core(g_mine), hi, swap_core(hi)]
    far = [near, swap_core(near), cross, swap_core(cross)]

    gw = call(gw_kernel, [(4, 640, 640)], WORK, 10)(at, *own, *far, context, c_far)[0]
    gw, weight = lax.optimization_barrier((gw, weight))
    gw = lax.psum_scatter(gw.reshape(8, 4, 80, 640), "blk", scatter_dimension=0, tiled=True)
    grad_weight = over_y(gw[0], y)

    w = weight.reshape(4, 640, 640)
    keep, give = call(proj_kernel, [(2, 2, 384, 640)] * 2, WORK, 3)(at, context, c_far, w)
    keep = add(keep, swap_core(give)).astype(BF)
    parts = keep, swap_hi(keep[1, 1]), swap_lo(keep[0, 0]), swap_both(keep[1, 0])
    projected = call(join_kernel, [(384, 1280)], 0, 4)(at, *parts)[0]

    gc_far, gc_own = call(gc_kernel, [(384, 640)] * 2, WORK, 9)(at, *own, *far, w)
    grad_context = add(gc_own, swap_lo(gc_far)).astype(BF)
    return projected, grad_context, grad_weight


def solution(mesh):
    spec = P(("blk", "rep"), "tp")
    return jax.shard_map(
        body,
        mesh=mesh,
        in_specs=(spec, P("blk", "tp"), spec),
        out_specs=(spec, spec, spec),
        check_vma=False,
    )
```

```python
import jax
import jax.numpy as jnp
from jax import lax
from jax.experimental import pallas as pl
from jax.experimental.pallas import tpu as pltpu
from jax.sharding import PartitionSpec as P

BF, F32 = jnp.bfloat16, jnp.float32
ALL = ("blk", "tp", "rep")
WORK = 2 * 768 * 2560 * 640


def number(z, a, k, l, y):
    return (z * 4 + a * 2 + k) * 8 + l * 4 + y


def places():
    for z in range(8):
        for a in range(2):
            for k in range(2):
                for l in range(2):
                    for y in range(4):
                        yield z, a, k, l, y


def move(value, target):
    return lax.ppermute(value, ALL, [(number(*p), number(*target(*p))) for p in places()])


def swap_core(v):
    return move(v, lambda z, a, k, l, y: (z, a, 1 - k, l, y))


def swap_lo(v):
    return move(v, lambda z, a, k, l, y: (z, a, k, 1 - l, y))


def swap_hi(v):
    return move(v, lambda z, a, k, l, y: (z, 1 - a, k, l, y))


def swap_both(v):
    return move(v, lambda z, a, k, l, y: (z, 1 - a, k, 1 - l, y))


def to_y(v, d):
    return move(v, lambda z, a, k, l, y: (z, a, k, l, (y + d) % 4))


def dot(a, b, ca, cb):
    return lax.dot_general(a, b, (((ca,), (cb,)), ((), ())), preferred_element_type=F32)


def add(*terms):
    total = terms[0].astype(F32)
    for term in terms[1:]:
        total = total + term.astype(F32)
    return total


def pick(v, i, axis):
    return lax.dynamic_index_in_dim(v, i, axis, keepdims=False)


def over_y(v, y):
    turn = (1, 3, 2)
    mine, *pieces = lax.optimization_barrier([pick(v, (y + d) % 4, 0) for d in (0, *turn)])
    return add(mine, *(to_y(piece, d) for piece, d in zip(pieces, turn)))


def call(kernel, outs, flops, n_in):
    whole = pl.BlockSpec(memory_space=pltpu.VMEM)
    return pl.pallas_call(
        kernel,
        out_shape=[jax.ShapeDtypeStruct(s, BF) for s in outs],
        in_specs=[pl.BlockSpec(memory_space=pltpu.SMEM)] + [whole] * n_in,
        out_specs=[whole] * len(outs),
        compiler_params=pltpu.CompilerParams(vmem_limit_bytes=40 << 20),
        cost_estimate=pl.CostEstimate(flops=flops, bytes_accessed=8 << 20, transcendentals=0),
    )


def split_kernel(at, g, mine, theirs):
    for f in range(2):

        @pl.when(at[1] == f)
        def _():
            for i in range(2):
                mine[:, i * 320 : i * 320 + 320] = g[:, i * 640 + f * 320 : i * 640 + f * 320 + 320]
                theirs[:, i * 320 : i * 320 + 320] = g[:, i * 640 + 320 - f * 320 : i * 640 + 640 - f * 320]


def join_kernel(at, keep, hi, lo, both, out):
    first = (keep[0, 1].astype(F32) + hi[...].astype(F32)).astype(BF)
    second = (lo[...].astype(F32) + both[...].astype(F32)).astype(BF)
    for f in range(2):

        @pl.when(at[1] == f)
        def _():
            for i in range(2):
                out[:, i * 640 + f * 320 : i * 640 + f * 320 + 320] = first[:, i * 320 : i * 320 + 320]
                out[:, i * 640 + 320 - f * 320 : i * 640 + 640 - f * 320] = second[:, i * 320 : i * 320 + 320]


def gw_kernel(at, *refs):
    g_own, g_far, c_own, c_far, out = refs[:4], refs[4:8], refs[8], refs[9], refs[10]
    for q in range(4):
        out[at[0] ^ q] = (dot(g_own[q][...], c_own[...], 0, 0) + dot(g_far[q][...], c_far[...], 0, 0)).astype(BF)


def proj_kernel(at, c_own, c_far, w, *outs):
    for q in (1, 3, 0, 2):
        for s, c in enumerate((c_far, c_own)):
            outs[q % 2][q // 2, s] = dot(c[...], w[at[0] ^ q], 1, 1).astype(BF)


def gc_kernel(at, *refs):
    w, far, own = refs[8:]
    for g, out in ((refs[4:8], far), (refs[:4], own)):
        total = dot(g[0][...], w[at[0]], 1, 0)
        for q in range(1, 4):
            total += dot(g[q][...], w[at[0] ^ q], 1, 0)
        out[...] = total.astype(BF)


def body(context, out_weight, grad_out):
    t = lax.axis_index("tp")
    r = lax.axis_index("rep")
    f, y = r // 4, r % 4
    at = jnp.stack([t, f]).astype(jnp.int32)

    half = lax.dynamic_slice_in_dim(out_weight, f * 320, 320, 0)
    weight = lax.all_gather(half, "blk", axis=0, tiled=True)

    c_far = swap_lo(context)
    g_mine, g_theirs = call(split_kernel, [(384, 640)] * 2, 0, 1)(at, grad_out)
    near = swap_lo(g_theirs)
    cross = swap_both(g_theirs)
    hi = swap_hi(g_mine)
    own = [g_mine, swap_core(g_mine), hi, swap_core(hi)]
    far = [near, swap_core(near), cross, swap_core(cross)]

    gw = call(gw_kernel, [(4, 640, 640)], WORK, 10)(at, *own, *far, context, c_far)[0]
    gw, weight = lax.optimization_barrier((gw, weight))
    gw = lax.psum_scatter(gw.reshape(8, 4, 80, 640), "blk", scatter_dimension=0, tiled=True)

    w = weight.reshape(4, 640, 640)
    keep, give = call(proj_kernel, [(2, 2, 384, 640)] * 2, WORK, 3)(at, context, c_far, w)
    keep = add(keep, swap_core(give)).astype(BF)
    parts = keep, swap_hi(keep[1, 1]), swap_lo(keep[0, 0]), swap_both(keep[1, 0])
    projected = call(join_kernel, [(384, 1280)], 0, 4)(at, *parts)[0]

    gc_far, gc_own = call(gc_kernel, [(384, 640)] * 2, WORK, 9)(at, *own, *far, w)
    grad_context = add(gc_own, swap_lo(gc_far)).astype(BF)
    gw, grad_context = lax.optimization_barrier((gw[0], grad_context))
    grad_weight = over_y(gw, y)
    return projected, grad_context, grad_weight


def solution(mesh):
    spec = P(("blk", "rep"), "tp")
    return jax.shard_map(
        body,
        mesh=mesh,
        in_specs=(spec, P("blk", "tp"), spec),
        out_specs=(spec, spec, spec),
        check_vma=False,
    )
```
